512 devices in a mesh: dp: 16 (over z, y_lo), tensor: 32 (over x, y_hi, core).
Axes of the slice: x: 4, y: 8 (y_hi: 4, y_lo: 2; y = y_hi * 2 + y_lo), z: 8, core: 2. Of those that a mesh axis runs over, the one named last changes fastest.
Arguments:
- activations: bfloat16 [2048, 8192], P('tensor', 'dp'), may hold values from -6 to 6
- grad_out: bfloat16 [2048, 28672], P('dp', 'tensor'), may hold values from -6 to 6
- weight: bfloat16 [8192, 28672], P('dp', 'tensor'), may hold values from -0.0625 to 0.0625
- block_mask: int32 [64, 224], P('dp', 'tensor'), may hold values from 0 to 1, as said below
Outputs:
- grad_input: bfloat16 [2048, 8192], P('tensor', 'dp')
- grad_weight: bfloat16 [8192, 28672], P('dp', 'tensor')
The draws below stay inside these ranges and needn't reach their ends.
Inputs may be any that keep to these rules, and one draw needn't show every extreme that they name: `block_mask`: each entry is 0 or 1; the share of ones differs from one column of blocks to the next and is a quarter on average.
All inputs are finite; a program needn't handle non-finite values.
Results may differ from the reference program's by a relative error of at most 0.019.
Values may be sent and summed in bfloat16 or wider, within the bound.
No kernel may reach another device: no remote copies, remote signals or barrier semaphores. Data moves between devices by JAX's collectives and lax.ppermute only.
A program may use at most 64 MiB of HBM per device.

```python
import math
import jax
import jax.numpy as jnp
from jax import lax

D = 8192
FF = 28672
BLK = 128
TOKENS = 2048
N_TENSOR = 32


def draw_block_mask(key, part):
    key = jax.random.fold_in(key, 5)
    level_key, entry_key = jax.random.split(key)
    levels = jax.random.randint(level_key, (FF // BLK,), 1, 8)
    entries = jax.random.randint(entry_key, (D // BLK, FF // BLK), 0, 16)
    return (entries < levels[None, :]).astype(jnp.int32)


def shard_levels(stream_key, dims, cuts, least, largest):
    factor_of = 1.0
    for dim, parts in cuts:
        steps = jax.random.uniform(jax.random.fold_in(jax.random.fold_in(stream_key, 6), dim), (parts,), jnp.float32, least / len(cuts), largest / len(cuts))
        factor_of = factor_of * jnp.repeat(jnp.exp(steps), dims[dim] // parts).reshape((-1,) + (1,) * (len(dims) - 1 - dim))
    return factor_of


def gaussian(rng, shape, scale, most, cuts=(), kind=jnp.bfloat16):
    result = scale * jax.random.normal(rng, shape, jnp.float32)
    if cuts:
        result = result * shard_levels(rng, shape, cuts, -0.22, 0.18)
    return jnp.clip(result, -most, most).astype(kind)


def setup_inputs(seed: int = 0) -> dict:
    splits = jax.random.split(jax.random.key(seed), 5)
    activations = gaussian(splits[0], (TOKENS, D), 1.0, 6.0, ((0, 32), (1, 16)))
    grad_out = gaussian(splits[1], (TOKENS, FF), 1.0, 6.0, ((0, 16), (1, 32)))
    weight = gaussian(splits[2], (D, FF), D ** -0.5, 0.0625, ((0, 16), (1, 32)))
    block_mask = draw_block_mask(jax.random.fold_in(splits[4], 71), 0)
    return {"activations": activations, "grad_out": grad_out, "weight": weight, "block_mask": block_mask}


def expand_mask(block_mask):
    rows, cols = block_mask.shape
    flags = block_mask.astype(jnp.bfloat16)
    spread = jnp.broadcast_to(flags[:, None, :, None], (rows, BLK, cols, BLK))
    return spread.reshape(rows * BLK, cols * BLK)

def reference(activations, grad_out, weight, block_mask):
    keep_mask = expand_mask(block_mask)
    masked = weight * keep_mask
    group = FF // N_TENSOR

    def add_group(total, index):
        start = (index * group).astype(jnp.int32)
        out_cols = lax.dynamic_slice_in_dim(grad_out, start, group, 1)
        weight_cols = lax.dynamic_slice_in_dim(masked, start, group, 1)
        group_sum = jnp.dot(out_cols, weight_cols.T, preferred_element_type=jnp.float32).astype(jnp.bfloat16)
        group_sum = lax.optimization_barrier(group_sum)
        return (total + group_sum.astype(jnp.float32), None)
    start_total = jnp.zeros((TOKENS, D), jnp.float32)
    input_sum, _ = lax.scan(add_group, start_total, jnp.arange(N_TENSOR, dtype=jnp.int32))
    grad_input = input_sum.astype(jnp.bfloat16)
    weight_sum = jnp.dot(activations.T, grad_out, preferred_element_type=jnp.float32)
    factor = 1.0 / math.sqrt(TOKENS)
    grad_weight = (weight_sum * keep_mask.astype(jnp.float32) * factor).astype(jnp.bfloat16)
    return (grad_input, grad_weight)
```

```python
import math

import jax
import jax.numpy as jnp
from jax import lax
from jax.sharding import Mesh, PartitionSpec as P

AXES = ("z", "y_lo", "x", "y_hi", "core")
SIZES = (8, 2, 4, 4, 2)
PLANE = ("x", "y_hi")
SWAP = ((0, 1), (1, 0))


def expand_mask(block_mask, side, dtype):
    rows, cols = block_mask.shape
    flags = block_mask.astype(dtype)
    spread = jnp.broadcast_to(flags[:, None, :, None], (rows, side, cols, side))
    return spread.reshape(rows * side, cols * side)


def matmul(a, b, contract):
    return lax.dot_general(a, b, ((contract[:1], contract[1:]), ((), ())), preferred_element_type=jnp.float32)


def shards(activations, grad_out, weight, block_mask):
    side = weight.shape[0] // block_mask.shape[0]
    hidden = weight.shape[1]
    rows = activations.shape[0]
    chips = lax.axis_size("x") * lax.axis_size("y_hi")
    core = lax.axis_index("core")

    both = lax.all_gather(grad_out, "core", axis=0)
    own = lax.dynamic_slice(grad_out, (core * rows, 0), (rows, hidden))
    other = lax.dynamic_slice(both, (1 - core, core * rows, 0), (1, rows, hidden))[0]
    pair = jnp.concatenate([own, other], axis=1)
    pair = lax.all_gather(pair, "y_lo", axis=0, tiled=True)
    whole_out = lax.all_gather(pair, "z", axis=0, tiled=True)
    tokens = whole_out.shape[0] * 2

    masked = weight * expand_mask(block_mask, side, jnp.bfloat16)
    masked = jnp.concatenate([masked, lax.ppermute(masked, "core", SWAP)], axis=1)
    copies = jnp.broadcast_to(activations[None], (chips,) + activations.shape)
    inputs = lax.all_to_all(copies, PLANE, 0, 0, tiled=True)
    inputs = inputs.reshape(chips * rows, -1)

    partial_value = matmul(whole_out, masked, (1, 1)).astype(jnp.bfloat16)
    parts = lax.all_to_all(partial_value.reshape(chips, rows, -1), PLANE, 0, 0, tiled=True)
    grad_input = jnp.sum(parts.astype(jnp.float32), axis=0).astype(jnp.bfloat16)

    theirs = matmul(inputs, whole_out[:, hidden:], (0, 0)).astype(jnp.bfloat16)
    theirs = lax.ppermute(theirs, "core", SWAP)
    weight_sum = matmul(inputs, whole_out[:, :hidden], (0, 0)) + theirs.astype(jnp.float32)
    factor = 1.0 / math.sqrt(tokens)
    grad_weight = (weight_sum * expand_mask(block_mask, side, jnp.float32) * factor).astype(jnp.bfloat16)
    return (grad_input, grad_weight)


def solution(mesh):
    fine = Mesh(mesh.devices.reshape(SIZES), AXES)
    dp, tensor = ("z", "y_lo"), ("x", "y_hi", "core")
    return jax.shard_map(
        shards,
        mesh=fine,
        in_specs=(P(tensor, dp), P(dp, tensor), P(dp, tensor), P(dp, tensor)),
        out_specs=(P(tensor, dp), P(dp, tensor)),
        check_vma=False,
    )
```

```python
import functools
import math

import jax
import jax.numpy as jnp
from jax import lax
from jax.experimental import pallas as pl
from jax.experimental.pallas import tpu as pltpu
from jax.sharding import Mesh, PartitionSpec as P

AXES = ("z", "y_lo", "x", "y_hi", "core")
SIZES = (8, 2, 4, 4, 2)
SWAP = ((0, 1), (1, 0))


def expand_mask(block_mask, side, dtype):
    rows, cols = block_mask.shape
    flags = block_mask.astype(dtype)
    spread = jnp.broadcast_to(flags[:, None, :, None], (rows, side, cols, side))
    return spread.reshape(rows * side, cols * side)


def matmul(a, b, contract):
    return lax.dot_general(a, b, ((contract[:1], contract[1:]), ((), ())), preferred_element_type=jnp.float32)


def near(place, size):
    return place ^ 1


def next_pair(place, size):
    return (((place - 1 + size) % size ^ 1) + 1) % size


def swap(value, axis, partner):
    size = lax.axis_size(axis)
    pairs = []
    for place in range(size):
        for core in range(2):
            there = (partner((place - core) % size, size) + core) % size
            pairs.append((place * 2 + core, there * 2 + core))
    return lax.ppermute(value, (axis, "core"), pairs)


def after(value, *done):
    return lax.optimization_barrier((value,) + done)[0]


def call(kernel, outs, args, n_scalar, scratch=()):
    scalar, vector = pl.BlockSpec(memory_space=pltpu.SMEM), pl.BlockSpec(memory_space=pltpu.VMEM)
    return pl.pallas_call(
        kernel,
        out_shape=[jax.ShapeDtypeStruct(shape, jnp.bfloat16) for shape in outs],
        in_specs=[scalar] * n_scalar + [vector] * (len(args) - n_scalar),
        out_specs=[vector] * len(outs),
        scratch_shapes=list(scratch),
        compiler_params=pltpu.CompilerParams(vmem_limit_bytes=24 * 2**20),
    )(*args)


def dot(a, b, contract):
    return lax.dot_general(a, b, ((contract[:1], contract[1:]), ((), ())), preferred_element_type=jnp.float32)


def block_at(index, rows):
    return pl.ds(pl.multiple_of(index * rows, rows), rows)


def place_kernel(order, *refs):
    parts, out = refs[:-1], refs[-1]
    rows = parts[0].shape[0] // 2
    for k, part in enumerate(parts):
        for i in range(2):
            out[block_at(order[2 * k + i], rows)] = part[i * rows : (i + 1) * rows]


def away_kernel(order, quad, *refs):
    parts, in_rows, away, held = refs[:-3], refs[-3], refs[-2], refs[-1]
    rows, hidden = quad.shape[1], away.shape[1]
    for k, part in enumerate(parts):
        held[2 * k * rows : (2 * k + 2) * rows] = part[:, hidden:]
        for i in range(2 * k, 2 * k + 2):
            in_rows[i * rows : (i + 1) * rows] = quad[order[i]]
    away[...] = dot(in_rows[...], held[...], (0, 0)).astype(jnp.bfloat16)


def home_kernel(factor, mask, in_rows, received, *refs):
    parts, out, held = refs[:-2], refs[-2], refs[-1]
    width, hidden = out.shape
    rows = parts[0].shape[0]
    for k, part in enumerate(parts):
        held[k * rows : (k + 1) * rows] = part[:, :hidden]
    height, side = width // mask.shape[0], hidden // mask.shape[1]
    total = dot(in_rows[...], held[...], (0, 0)) + received[...].astype(jnp.float32)
    for i in range(mask.shape[0]):
        for j in range(mask.shape[1]):
            keep = mask[i, j].astype(jnp.float32)
            block = total[i * height : (i + 1) * height, j * side : (j + 1) * side]
            out[i * height : (i + 1) * height, j * side : (j + 1) * side] = (block * keep * factor).astype(jnp.bfloat16)


def shards(activations, grad_out, weight, block_mask):
    side = weight.shape[0] // block_mask.shape[0]
    width, hidden = weight.shape
    rows = activations.shape[0]
    core = lax.axis_index("core")
    z, r = lax.axis_index("z"), lax.axis_index("y_lo")

    here = (z - core) % 8
    other, one = here ^ 1, next_pair(here, 8)
    two, far = next_pair(other, 8), next_pair(one ^ 1, 8)
    ring = [here, other, one, one ^ 1, two, two ^ 1, far, far ^ 1]
    three = two ^ 1
    ring += [here, one, other, two, one ^ 1, next_pair(one ^ 1, 8), three, next_pair(three, 8)]
    spots = [(s + core) % 8 for s in ring]
    chips = [spot // 2 * 4 + spot % 2 * 2 + (r if i < 8 else 1 - r) for i, spot in enumerate(spots)]
    order = jnp.stack(chips).astype(jnp.int32)

    both = lax.all_gather(grad_out, "core", axis=0)
    own = lax.dynamic_slice(grad_out, (core * rows, 0), (rows, hidden))
    sibling = lax.dynamic_slice(both, (1 - core, core * rows, 0), (1, rows, hidden))[0]
    first = jnp.concatenate([own, sibling], axis=1)

    across = lax.ppermute(first, "y_lo", SWAP)
    a1 = swap(first, "z", near)
    a1 = jnp.concatenate([first, a1], axis=0)
    a2 = swap(a1, "z", next_pair)
    b1 = swap(across, "z", next_pair)
    b1 = jnp.concatenate([across, b1], axis=0)
    masked = after(weight, across) * expand_mask(block_mask, side, jnp.bfloat16)
    wide = jnp.concatenate([masked, lax.ppermute(masked, "core", SWAP)], axis=1)
    wide = lax.optimization_barrier(wide)
    b2 = swap(b1, "z", near)
    copies = jnp.broadcast_to(after(activations, a1)[None], (16,) + activations.shape)
    quad = lax.all_to_all(copies, ("x", "y_hi"), 0, 0, tiled=True)
    a3 = swap(a2, "z", near)
    b3 = swap(b2, "z", next_pair)
    a4 = swap(a3, "z", next_pair)
    b4 = swap(b3, "z", near)

    parts = (a1, a2, a3, a4, b1, b2, b3, b4)
    value = [matmul(part, wide, (1, 1)).astype(jnp.bfloat16) for part in parts]
    (value,) = call(place_kernel, [(16 * rows, width)], (order, *value), 1)
    value = lax.all_to_all(value.reshape(16, rows, width), ("x", "y_hi"), 0, 0, tiled=True)
    grad_input = jnp.sum(value.astype(jnp.float32), axis=0).astype(jnp.bfloat16)

    scratch = [pltpu.VMEM((16 * rows, hidden), jnp.bfloat16)]
    in_rows, away = call(away_kernel, [(16 * rows, width), (width, hidden)], (order, quad, *parts), 1, scratch)
    received = lax.ppermute(away, "core", SWAP)
    factor = 1.0 / math.sqrt(rows * 32)
    home = functools.partial(home_kernel, factor)
    (grad_weight,) = call(home, [(width, hidden)], (block_mask, in_rows, received, *parts), 1, scratch)
    return (grad_input, grad_weight)


def solution(mesh):
    fine = Mesh(mesh.devices.reshape(SIZES), AXES)
    dp, tensor = ("z", "y_lo"), ("x", "y_hi", "core")
    return jax.shard_map(
        shards,
        mesh=fine,
        in_specs=(P(tensor, dp), P(dp, tensor), P(dp, tensor), P(dp, tensor)),
        out_specs=(P(tensor, dp), P(dp, tensor)),
        check_vma=False,
    )
```

```python
import functools
import math

import jax
import jax.numpy as jnp
from jax import lax
from jax.experimental import pallas as pl
from jax.experimental.pallas import tpu as pltpu
from jax.sharding import Mesh, PartitionSpec as P

AXES = ("z", "y_lo", "x", "y_hi", "core")
SIZES = (8, 2, 4, 4, 2)
SWAP = ((0, 1), (1, 0))


def expand_mask(block_mask, side, dtype):
    rows, cols = block_mask.shape
    flags = block_mask.astype(dtype)
    spread = jnp.broadcast_to(flags[:, None, :, None], (rows, side, cols, side))
    return spread.reshape(rows * side, cols * side)


def matmul(a, b, contract):
    return lax.dot_general(a, b, ((contract[:1], contract[1:]), ((), ())), preferred_element_type=jnp.float32)


def near(place, size):
    return place ^ 1


def next_pair(place, size):
    return (((place - 1 + size) % size ^ 1) + 1) % size


def swap(value, axis, partner):
    size = lax.axis_size(axis)
    pairs = []
    for place in range(size):
        for core in range(2):
            there = (partner((place - core) % size, size) + core) % size
            pairs.append((place * 2 + core, there * 2 + core))
    return lax.ppermute(value, (axis, "core"), pairs)


def after(value, *done):
    return lax.optimization_barrier((value,) + done)[0]


def call(kernel, outs, args, n_scalar, scratch=()):
    scalar, vector = pl.BlockSpec(memory_space=pltpu.SMEM), pl.BlockSpec(memory_space=pltpu.VMEM)
    return pl.pallas_call(
        kernel,
        out_shape=[jax.ShapeDtypeStruct(shape, jnp.bfloat16) for shape in outs],
        in_specs=[scalar] * n_scalar + [vector] * (len(args) - n_scalar),
        out_specs=[vector] * len(outs),
        scratch_shapes=list(scratch),
        compiler_params=pltpu.CompilerParams(vmem_limit_bytes=24 * 2**20),
    )(*args)


def dot(a, b, contract):
    return lax.dot_general(a, b, ((contract[:1], contract[1:]), ((), ())), preferred_element_type=jnp.float32)


def block_at(index, rows):
    return pl.ds(pl.multiple_of(index * rows, rows), rows)


def place_kernel(order, *refs):
    parts, out = refs[:-1], refs[-1]
    rows = parts[0].shape[0] // 4
    for k, part in enumerate(parts):
        for i in range(4):
            out[block_at(order[4 * k + i], rows)] = part[i * rows : (i + 1) * rows]


def away_kernel(order, quad, *refs):
    parts, in_rows, away, held = refs[:-3], refs[-3], refs[-2], refs[-1]
    rows, hidden = quad.shape[1], away.shape[1]
    for k, part in enumerate(parts):
        held[4 * k * rows : (4 * k + 4) * rows] = part[:, hidden:]
        for i in range(4 * k, 4 * k + 4):
            in_rows[i * rows : (i + 1) * rows] = quad[order[i]]
    away[...] = dot(in_rows[...], held[...], (0, 0)).astype(jnp.bfloat16)


def home_kernel(factor, mask, in_rows, received, *refs):
    parts, out, held = refs[:-2], refs[-2], refs[-1]
    width, hidden = out.shape
    rows = parts[0].shape[0]
    for k, part in enumerate(parts):
        held[k * rows : (k + 1) * rows] = part[:, :hidden]
    height, side = width // mask.shape[0], hidden // mask.shape[1]
    total = dot(in_rows[...], held[...], (0, 0)) + received[...].astype(jnp.float32)
    for i in range(mask.shape[0]):
        for j in range(mask.shape[1]):
            keep = mask[i, j].astype(jnp.float32)
            block = total[i * height : (i + 1) * height, j * side : (j + 1) * side]
            out[i * height : (i + 1) * height, j * side : (j + 1) * side] = (block * keep * factor).astype(jnp.bfloat16)


def shards(activations, grad_out, weight, block_mask):
    side = weight.shape[0] // block_mask.shape[0]
    width, hidden = weight.shape
    rows = activations.shape[0]
    core = lax.axis_index("core")
    z, r = lax.axis_index("z"), lax.axis_index("y_lo")

    here = (z - core) % 8
    other, one = here ^ 1, next_pair(here, 8)
    two, far = next_pair(other, 8), next_pair(one ^ 1, 8)
    ring = (here, other, one, one ^ 1, two, two ^ 1, far, far ^ 1)
    spots = [(s + core) % 8 for s in ring]
    chips = [spot // 2 * 4 + spot % 2 * 2 + (r ^ i) for spot in spots for i in range(2)]
    order = jnp.stack(chips).astype(jnp.int32)

    both = lax.all_gather(grad_out, "core", axis=0)
    own = lax.dynamic_slice(grad_out, (core * rows, 0), (rows, hidden))
    sibling = lax.dynamic_slice(both, (1 - core, core * rows, 0), (1, rows, hidden))[0]
    first = jnp.concatenate([own, sibling], axis=1)

    first = jnp.concatenate([first, lax.ppermute(first, "y_lo", SWAP)], axis=0)
    second = swap(first, "z", near)
    masked = after(weight, first) * expand_mask(block_mask, side, jnp.bfloat16)
    wide = jnp.concatenate([masked, lax.ppermute(masked, "core", SWAP)], axis=1)
    wide = lax.optimization_barrier(wide)
    pair = jnp.concatenate([first, second], axis=0)
    third = swap(pair, "z", next_pair)
    copies = jnp.broadcast_to(after(activations, third)[None], (16,) + activations.shape)
    quad = lax.all_to_all(copies, ("x", "y_hi"), 0, 0, tiled=True)
    fourth = swap(after(third, wide), "z", near)
    fifth = swap(fourth, "z", next_pair)

    parts = (pair, third, fourth, fifth)
    value = [matmul(part, wide, (1, 1)).astype(jnp.bfloat16) for part in parts]
    (value,) = call(place_kernel, [(16 * rows, width)], (order, *value), 1)
    value = lax.all_to_all(value.reshape(16, rows, width), ("x", "y_hi"), 0, 0, tiled=True)
    grad_input = jnp.sum(value.astype(jnp.float32), axis=0).astype(jnp.bfloat16)

    scratch = [pltpu.VMEM((16 * rows, hidden), jnp.bfloat16)]
    in_rows, away = call(away_kernel, [(16 * rows, width), (width, hidden)], (order, quad, *parts), 1, scratch)
    received = lax.ppermute(away, "core", SWAP)
    factor = 1.0 / math.sqrt(rows * 32)
    home = functools.partial(home_kernel, factor)
    (grad_weight,) = call(home, [(width, hidden)], (block_mask, in_rows, received, *parts), 1, scratch)
    return (grad_input, grad_weight)


def solution(mesh):
    fine = Mesh(mesh.devices.reshape(SIZES), AXES)
    dp, tensor = ("z", "y_lo"), ("x", "y_hi", "core")
    return jax.shard_map(
        shards,
        mesh=fine,
        in_specs=(P(tensor, dp), P(dp, tensor), P(dp, tensor), P(dp, tensor)),
        out_specs=(P(tensor, dp), P(dp, tensor)),
        check_vma=False,
    )
```

```python
import functools
import math

import jax
import jax.numpy as jnp
from jax import lax
from jax.experimental import pallas as pl
from jax.experimental.pallas import tpu as pltpu
from jax.sharding import Mesh, PartitionSpec as P

AXES = ("z", "y_lo", "x", "y_hi", "core")
SIZES = (8, 2, 4, 4, 2)
SWAP = ((0, 1), (1, 0))


def expand_mask(block_mask, side, dtype):
    rows, cols = block_mask.shape
    flags = block_mask.astype(dtype)
    spread = jnp.broadcast_to(flags[:, None, :, None], (rows, side, cols, side))
    return spread.reshape(rows * side, cols * side)


def matmul(a, b, contract):
    return lax.dot_general(a, b, ((contract[:1], contract[1:]), ((), ())), preferred_element_type=jnp.float32)


def near(place, size):
    return place ^ 1


def next_pair(place, size):
    return (((place - 1 + size) % size ^ 1) + 1) % size


def swap(value, axis, partner):
    size = lax.axis_size(axis)
    pairs = []
    for place in range(size):
        for core in range(2):
            there = (partner((place - core) % size, size) + core) % size
            pairs.append((place * 2 + core, there * 2 + core))
    return lax.ppermute(value, (axis, "core"), pairs)


def all_copies(value, axis):
    copies = jnp.broadcast_to(value[None], (lax.axis_size(axis),) + value.shape)
    return lax.all_to_all(copies, axis, 0, 0, tiled=True).reshape((-1,) + value.shape[1:])


def after(value, *done):
    return lax.optimization_barrier((value,) + done)[0]


def call(kernel, outs, args, n_scalar, scratch=()):
    scalar, vector = pl.BlockSpec(memory_space=pltpu.SMEM), pl.BlockSpec(memory_space=pltpu.VMEM)
    return pl.pallas_call(
        kernel,
        out_shape=[jax.ShapeDtypeStruct(shape, jnp.bfloat16) for shape in outs],
        in_specs=[scalar] * n_scalar + [vector] * (len(args) - n_scalar),
        out_specs=[vector] * len(outs),
        scratch_shapes=list(scratch),
        compiler_params=pltpu.CompilerParams(vmem_limit_bytes=24 * 2**20),
    )(*args)


def dot(a, b, contract):
    return lax.dot_general(a, b, ((contract[:1], contract[1:]), ((), ())), preferred_element_type=jnp.float32)


def block_at(index, rows):
    return pl.ds(pl.multiple_of(index * rows, rows), rows)


def place_kernel(order, *refs):
    parts, out = refs[:-1], refs[-1]
    rows = parts[0].shape[0] // 2
    for k, part in enumerate(parts):
        for i in range(2):
            out[block_at(order[2 * k + i], rows)] = part[i * rows : (i + 1) * rows]


def away_kernel(order, quad, *refs):
    parts, in_rows, away, held = refs[:-3], refs[-3], refs[-2], refs[-1]
    rows, hidden = quad.shape[1], away.shape[1]
    for k, part in enumerate(parts):
        held[2 * k * rows : (2 * k + 2) * rows] = part[:, hidden:]
        for i in range(2 * k, 2 * k + 2):
            in_rows[i * rows : (i + 1) * rows] = quad[order[i]]
    away[...] = dot(in_rows[...], held[...], (0, 0)).astype(jnp.bfloat16)


def home_kernel(factor, mask, in_rows, received, *refs):
    parts, out, held = refs[:-2], refs[-2], refs[-1]
    width, hidden = out.shape
    rows = parts[0].shape[0]
    for k, part in enumerate(parts):
        held[k * rows : (k + 1) * rows] = part[:, :hidden]
    height, side = width // mask.shape[0], hidden // mask.shape[1]
    total = dot(in_rows[...], held[...], (0, 0)) + received[...].astype(jnp.float32)
    for i in range(mask.shape[0]):
        for j in range(mask.shape[1]):
            keep = mask[i, j].astype(jnp.float32)
            block = total[i * height : (i + 1) * height, j * side : (j + 1) * side]
            out[i * height : (i + 1) * height, j * side : (j + 1) * side] = (block * keep * factor).astype(jnp.bfloat16)


def shards(activations, grad_out, weight, block_mask):
    side = weight.shape[0] // block_mask.shape[0]
    width, hidden = weight.shape
    rows = activations.shape[0]
    core = lax.axis_index("core")
    z, r = lax.axis_index("z"), lax.axis_index("y_lo")

    here = (z - core) % 8
    other, one = here ^ 1, next_pair(here, 8)
    two, far = next_pair(other, 8), next_pair(one ^ 1, 8)
    spots = [(s + core) % 8 for s in (here, other, one, one ^ 1, two, two ^ 1, far, far ^ 1)]
    chips = [spot // 2 * 4 + spot % 2 * 2 + half for half in (r, 1 - r) for spot in spots]
    order = jnp.stack(chips).astype(jnp.int32)

    both = lax.all_gather(grad_out, "core", axis=0)
    own = lax.dynamic_slice(grad_out, (core * rows, 0), (rows, hidden))
    sibling = lax.dynamic_slice(both, (1 - core, core * rows, 0), (1, rows, hidden))[0]
    first = jnp.concatenate([own, sibling], axis=1)

    b0 = lax.ppermute(first, "y_lo", SWAP)
    a1 = swap(first, "z", near)
    line = all_copies(after(activations, first), "y_hi")
    pair = jnp.concatenate([first, a1], axis=0)
    a2 = swap(pair, "z", next_pair)
    b1 = lax.ppermute(a1, "y_lo", SWAP)
    masked = after(weight, a1) * expand_mask(block_mask, side, jnp.bfloat16)
    wide = jnp.concatenate([masked, lax.ppermute(masked, "core", SWAP)], axis=1)
    wide = lax.optimization_barrier(wide)
    b2 = lax.ppermute(a2, "y_lo", SWAP)
    a3 = swap(a2, "z", near)
    quad = all_copies(after(line, a2, b1), "x").reshape(16, rows, width)
    b3 = swap(after(b2, wide), "z", near)
    a4 = swap(a3, "z", next_pair)
    b4 = swap(b3, "z", next_pair)

    parts = (pair, a2, a3, a4, jnp.concatenate([b0, b1], axis=0), b2, b3, b4)
    value = [matmul(part, wide, (1, 1)).astype(jnp.bfloat16) for part in parts]
    (value,) = call(place_kernel, [(16 * rows, width)], (order, *value), 1)
    value = lax.all_to_all(value.reshape(16, rows, width), ("x", "y_hi"), 0, 0, tiled=True)
    scratch = [pltpu.VMEM((16 * rows, hidden), jnp.bfloat16)]
    in_rows, away = call(away_kernel, [(16 * rows, width), (width, hidden)], (order, quad, *parts), 1, scratch)
    received = lax.ppermute(away, "core", SWAP)
    factor = 1.0 / math.sqrt(rows * 32)
    home = functools.partial(home_kernel, factor)
    (grad_weight,) = call(home, [(width, hidden)], (block_mask, in_rows, received, *parts), 1, scratch)
    grad_input = jnp.sum(after(value, grad_weight).astype(jnp.float32), axis=0).astype(jnp.bfloat16)
    return (grad_input, grad_weight)


def solution(mesh):
    fine = Mesh(mesh.devices.reshape(SIZES), AXES)
    dp, tensor = ("z", "y_lo"), ("x", "y_hi", "core")
    return jax.shard_map(
        shards,
        mesh=fine,
        in_specs=(P(tensor, dp), P(dp, tensor), P(dp, tensor), P(dp, tensor)),
        out_specs=(P(tensor, dp), P(dp, tensor)),
        check_vma=False,
    )
```

```python
import functools
import math

import jax
import jax.numpy as jnp
from jax import lax
from jax.experimental import pallas as pl
from jax.experimental.pallas import tpu as pltpu
from jax.sharding import Mesh, PartitionSpec as P

AXES = ("z", "y_lo", "x", "y_hi", "core")
SIZES = (8, 2, 4, 4, 2)
SWAP = ((0, 1), (1, 0))


def expand_mask(block_mask, side, dtype):
    rows, cols = block_mask.shape
    flags = block_mask.astype(dtype)
    spread = jnp.broadcast_to(flags[:, None, :, None], (rows, side, cols, side))
    return spread.reshape(rows * side, cols * side)


def matmul(a, b, contract):
    return lax.dot_general(a, b, ((contract[:1], contract[1:]), ((), ())), preferred_element_type=jnp.float32)


def near(place, size):
    return place ^ 1


def next_pair(place, size):
    return (((place - 1 + size) % size ^ 1) + 1) % size


def swap(value, axis, partner):
    size = lax.axis_size(axis)
    pairs = []
    for place in range(size):
        for core in range(2):
            there = (partner((place - core) % size, size) + core) % size
            pairs.append((place * 2 + core, there * 2 + core))
    return lax.ppermute(value, (axis, "core"), pairs)


def all_copies(value, axis):
    copies = jnp.broadcast_to(value[None], (lax.axis_size(axis),) + value.shape)
    return lax.all_to_all(copies, axis, 0, 0, tiled=True).reshape((-1,) + value.shape[1:])


def after(value, *done):
    return lax.optimization_barrier((value,) + done)[0]


def call(kernel, outs, args, n_scalar, scratch=()):
    scalar, vector = pl.BlockSpec(memory_space=pltpu.SMEM), pl.BlockSpec(memory_space=pltpu.VMEM)
    return pl.pallas_call(
        kernel,
        out_shape=[jax.ShapeDtypeStruct(shape, jnp.bfloat16) for shape in outs],
        in_specs=[scalar] * n_scalar + [vector] * (len(args) - n_scalar),
        out_specs=[vector] * len(outs),
        scratch_shapes=list(scratch),
        compiler_params=pltpu.CompilerParams(vmem_limit_bytes=24 * 2**20),
    )(*args)


def dot(a, b, contract):
    return lax.dot_general(a, b, ((contract[:1], contract[1:]), ((), ())), preferred_element_type=jnp.float32)


def block_at(index, rows):
    return pl.ds(pl.multiple_of(index * rows, rows), rows)


def place_kernel(order, *refs):
    parts, out = refs[:-1], refs[-1]
    rows = parts[0].shape[0] // 2
    for k, part in enumerate(parts):
        for i in range(2):
            out[block_at(order[2 * k + i], rows)] = part[i * rows : (i + 1) * rows]


def away_kernel(order, quad, *refs):
    parts, in_rows, away, held = refs[:-3], refs[-3], refs[-2], refs[-1]
    rows, hidden = quad.shape[1], away.shape[1]
    for k, part in enumerate(parts):
        held[2 * k * rows : (2 * k + 2) * rows] = part[:, hidden:]
        for i in range(2 * k, 2 * k + 2):
            in_rows[i * rows : (i + 1) * rows] = quad[order[i]]
    away[...] = dot(in_rows[...], held[...], (0, 0)).astype(jnp.bfloat16)


def home_kernel(factor, mask, in_rows, received, *refs):
    parts, out, held = refs[:-2], refs[-2], refs[-1]
    width, hidden = out.shape
    rows = parts[0].shape[0]
    for k, part in enumerate(parts):
        held[k * rows : (k + 1) * rows] = part[:, :hidden]
    height, side = width // mask.shape[0], hidden // mask.shape[1]
    total = dot(in_rows[...], held[...], (0, 0)) + received[...].astype(jnp.float32)
    for i in range(mask.shape[0]):
        for j in range(mask.shape[1]):
            keep = mask[i, j].astype(jnp.float32)
            block = total[i * height : (i + 1) * height, j * side : (j + 1) * side]
            out[i * height : (i + 1) * height, j * side : (j + 1) * side] = (block * keep * factor).astype(jnp.bfloat16)


def shards(activations, grad_out, weight, block_mask):
    side = weight.shape[0] // block_mask.shape[0]
    width, hidden = weight.shape
    rows = activations.shape[0]
    core = lax.axis_index("core")
    z, r = lax.axis_index("z"), lax.axis_index("y_lo")

    here = (z - core) % 8
    other, one = here ^ 1, next_pair(here, 8)
    two, far = next_pair(other, 8), next_pair(one ^ 1, 8)
    spots = [(s + core) % 8 for s in (here, other, one, one ^ 1, two, two ^ 1, far, far ^ 1)]
    chips = [spot // 2 * 4 + spot % 2 * 2 + half for half in (r, 1 - r) for spot in spots]
    order = jnp.stack(chips).astype(jnp.int32)

    both = lax.all_gather(grad_out, "core", axis=0)
    own = lax.dynamic_slice(grad_out, (core * rows, 0), (rows, hidden))
    sibling = lax.dynamic_slice(both, (1 - core, core * rows, 0), (1, rows, hidden))[0]
    first = jnp.concatenate([own, sibling], axis=1)

    b0 = lax.ppermute(first, "y_lo", SWAP)
    a1 = swap(first, "z", near)
    line = all_copies(after(activations, first), "y_hi")
    pair = jnp.concatenate([first, a1], axis=0)
    a2 = swap(pair, "z", next_pair)
    b1 = lax.ppermute(a1, "y_lo", SWAP)
    masked = after(weight, a1) * expand_mask(block_mask, side, jnp.bfloat16)
    wide = jnp.concatenate([masked, lax.ppermute(masked, "core", SWAP)], axis=1)
    wide = lax.optimization_barrier(wide)
    b2 = lax.ppermute(a2, "y_lo", SWAP)
    a3 = swap(a2, "z", near)
    quad = all_copies(after(line, a2), "x").reshape(16, rows, width)
    b3 = swap(after(b2, wide), "z", near)
    a4 = swap(a3, "z", next_pair)
    b4 = swap(b3, "z", next_pair)

    parts = (pair, a2, a3, a4, jnp.concatenate([after(b0, b3), after(b1, b3)], axis=0), b2, b3, b4)
    value = [matmul(part, wide, (1, 1)).astype(jnp.bfloat16) for part in parts]
    (value,) = call(place_kernel, [(16 * rows, width)], (order, *value), 1)
    value = lax.all_to_all(value.reshape(16, rows, width), ("x", "y_hi"), 0, 0, tiled=True)
    scratch = [pltpu.VMEM((16 * rows, hidden), jnp.bfloat16)]
    in_rows, away = call(away_kernel, [(16 * rows, width), (width, hidden)], (order, quad, *parts), 1, scratch)
    received = lax.ppermute(away, "core", SWAP)
    factor = 1.0 / math.sqrt(rows * 32)
    home = functools.partial(home_kernel, factor)
    (grad_weight,) = call(home, [(width, hidden)], (block_mask, in_rows, received, *parts), 1, scratch)
    grad_input = jnp.sum(after(value, grad_weight).astype(jnp.float32), axis=0).astype(jnp.bfloat16)
    return (grad_input, grad_weight)


def solution(mesh):
    fine = Mesh(mesh.devices.reshape(SIZES), AXES)
    dp, tensor = ("z", "y_lo"), ("x", "y_hi", "core")
    return jax.shard_map(
        shards,
        mesh=fine,
        in_specs=(P(tensor, dp), P(dp, tensor), P(dp, tensor), P(dp, tensor)),
        out_specs=(P(tensor, dp), P(dp, tensor)),
        check_vma=False,
    )
```

```python
import functools
import math

import jax
import jax.numpy as jnp
from jax import lax
from jax.experimental import pallas as pl
from jax.experimental.pallas import tpu as pltpu
from jax.sharding import Mesh, PartitionSpec as P

AXES = ("z", "y_lo", "x", "y_hi", "core")
SIZES = (8, 2, 4, 4, 2)
SWAP = ((0, 1), (1, 0))


def expand_mask(block_mask, side, dtype):
    rows, cols = block_mask.shape
    flags = block_mask.astype(dtype)
    spread = jnp.broadcast_to(flags[:, None, :, None], (rows, side, cols, side))
    return spread.reshape(rows * side, cols * side)


def matmul(a, b, contract):
    return lax.dot_general(a, b, ((contract[:1], contract[1:]), ((), ())), preferred_element_type=jnp.float32)


def near(place, size):
    return place ^ 1


def next_pair(place, size):
    return (((place - 1 + size) % size ^ 1) + 1) % size


def swap(value, axis, partner):
    size = lax.axis_size(axis)
    pairs = []
    for place in range(size):
        for core in range(2):
            there = (partner((place - core) % size, size) + core) % size
            pairs.append((place * 2 + core, there * 2 + core))
    return lax.ppermute(value, (axis, "core"), pairs)


def all_copies(value, axis):
    copies = jnp.broadcast_to(value[None], (lax.axis_size(axis),) + value.shape)
    return lax.all_to_all(copies, axis, 0, 0, tiled=True).reshape((-1,) + value.shape[1:])


def after(value, *done):
    return lax.optimization_barrier((value,) + done)[0]


def call(kernel, outs, args, n_scalar, scratch=()):
    scalar, vector = pl.BlockSpec(memory_space=pltpu.SMEM), pl.BlockSpec(memory_space=pltpu.VMEM)
    return pl.pallas_call(
        kernel,
        out_shape=[jax.ShapeDtypeStruct(shape, jnp.bfloat16) for shape in outs],
        in_specs=[scalar] * n_scalar + [vector] * (len(args) - n_scalar),
        out_specs=[vector] * len(outs),
        scratch_shapes=list(scratch),
        compiler_params=pltpu.CompilerParams(vmem_limit_bytes=24 * 2**20),
    )(*args)


def dot(a, b, contract):
    return lax.dot_general(a, b, ((contract[:1], contract[1:]), ((), ())), preferred_element_type=jnp.float32)


def block_at(index, rows):
    return pl.ds(pl.multiple_of(index * rows, rows), rows)


def place_kernel(order, *refs):
    parts, out = refs[:-1], refs[-1]
    rows = parts[0].shape[0] // 2
    for k, part in enumerate(parts):
        for i in range(2):
            out[block_at(order[2 * k + i], rows)] = part[i * rows : (i + 1) * rows]


def away_kernel(order, quad, *refs):
    parts, in_rows, away, held = refs[:-3], refs[-3], refs[-2], refs[-1]
    rows, hidden = quad.shape[1], away.shape[1]
    for k, part in enumerate(parts):
        held[2 * k * rows : (2 * k + 2) * rows] = part[:, hidden:]
        for i in range(2 * k, 2 * k + 2):
            in_rows[i * rows : (i + 1) * rows] = quad[order[i]]
    away[...] = dot(in_rows[...], held[...], (0, 0)).astype(jnp.bfloat16)


def home_kernel(factor, mask, in_rows, received, *refs):
    parts, out, held = refs[:-2], refs[-2], refs[-1]
    width, hidden = out.shape
    rows = parts[0].shape[0]
    for k, part in enumerate(parts):
        held[k * rows : (k + 1) * rows] = part[:, :hidden]
    height, side = width // mask.shape[0], hidden // mask.shape[1]
    total = dot(in_rows[...], held[...], (0, 0)) + received[...].astype(jnp.float32)
    for i in range(mask.shape[0]):
        for j in range(mask.shape[1]):
            keep = mask[i, j].astype(jnp.float32)
            block = total[i * height : (i + 1) * height, j * side : (j + 1) * side]
            out[i * height : (i + 1) * height, j * side : (j + 1) * side] = (block * keep * factor).astype(jnp.bfloat16)


def shards(activations, grad_out, weight, block_mask):
    side = weight.shape[0] // block_mask.shape[0]
    width, hidden = weight.shape
    rows = activations.shape[0]
    core = lax.axis_index("core")
    z, r = lax.axis_index("z"), lax.axis_index("y_lo")

    here = (z - core) % 8
    other, one = here ^ 1, next_pair(here, 8)
    two, far = next_pair(other, 8), next_pair(one ^ 1, 8)
    spots = [(s + core) % 8 for s in (here, other, one, one ^ 1, two, two ^ 1, far, far ^ 1)]
    chips = [spot // 2 * 4 + spot % 2 * 2 + half for half in (r, 1 - r) for spot in spots]
    order = jnp.stack(chips).astype(jnp.int32)

    both = lax.all_gather(grad_out, "core", axis=0)
    own = lax.dynamic_slice(grad_out, (core * rows, 0), (rows, hidden))
    sibling = lax.dynamic_slice(both, (1 - core, core * rows, 0), (1, rows, hidden))[0]
    first = jnp.concatenate([own, sibling], axis=1)

    b0 = lax.ppermute(first, "y_lo", SWAP)
    a1 = swap(first, "z", near)
    line = all_copies(after(activations, first), "y_hi")
    pair = jnp.concatenate([first, a1], axis=0)
    a2 = swap(pair, "z", next_pair)
    b1 = lax.ppermute(a1, "y_lo", SWAP)
    masked = after(weight, a1) * expand_mask(block_mask, side, jnp.bfloat16)
    wide = jnp.concatenate([masked, lax.ppermute(masked, "core", SWAP)], axis=1)
    wide = lax.optimization_barrier(wide)
    b2 = lax.ppermute(a2, "y_lo", SWAP)
    a3 = swap(a2, "z", near)
    quad = all_copies(after(line, a2), "x").reshape(16, rows, width)
    b3 = swap(after(b2, wide), "z", near)
    a4 = swap(a3, "z", next_pair)
    b4 = swap(b3, "z", next_pair)

    parts = (pair, a2, a3, a4, jnp.concatenate([b0, after(b1, b3)], axis=0), b2, b3, b4)
    value = [matmul(part, wide, (1, 1)).astype(jnp.bfloat16) for part in parts]
    (value,) = call(place_kernel, [(16 * rows, width)], (order, *value), 1)
    value = lax.all_to_all(value.reshape(16, rows, width), ("x", "y_hi"), 0, 0, tiled=True)
    scratch = [pltpu.VMEM((16 * rows, hidden), jnp.bfloat16)]
    in_rows, away = call(away_kernel, [(16 * rows, width), (width, hidden)], (order, quad, *parts), 1, scratch)
    received = lax.ppermute(away, "core", SWAP)
    factor = 1.0 / math.sqrt(rows * 32)
    home = functools.partial(home_kernel, factor)
    (grad_weight,) = call(home, [(width, hidden)], (block_mask, in_rows, received, *parts), 1, scratch)
    grad_input = jnp.sum(after(value, grad_weight).astype(jnp.float32), axis=0).astype(jnp.bfloat16)
    return (grad_input, grad_weight)


def solution(mesh):
    fine = Mesh(mesh.devices.reshape(SIZES), AXES)
    dp, tensor = ("z", "y_lo"), ("x", "y_hi", "core")
    return jax.shard_map(
        shards,
        mesh=fine,
        in_specs=(P(tensor, dp), P(dp, tensor), P(dp, tensor), P(dp, tensor)),
        out_specs=(P(tensor, dp), P(dp, tensor)),
        check_vma=False,
    )
```
